32 devices in a mesh: dp: 4 (over x, core), seq: 8 (over z, y).
Axes of the slice: x: 2, y: 2, z: 4, core: 2. Of those that a mesh axis runs over, the one named last changes fastest.
Arguments:
- tokens: bfloat16 [4, 16384, 1024], P('dp', 'seq'), may hold values from -6 to 6
- cotangent: bfloat16 [4, 16384, 1024], P('dp', 'seq'), may hold values from -6 to 6
- gain_mix: float32 [1024], replicated, may hold values from 0.25 to 1.75
- gain_mlp: float32 [1024], replicated, may hold values from 0.25 to 1.75
- fine_factor: bfloat16 [8, 128, 128], replicated, may hold values from -3.2 to 3.2, as said below
- coarse_factor: bfloat16 [8, 128, 128], replicated, may hold values from -3.2 to 3.2, as said below
- w_gate_up: bfloat16 [1024, 2048], P(('dp', 'seq')), may hold values from -0.1875 to 0.1875
- w_down: bfloat16 [1024, 1024], P(('dp', 'seq')), may hold values from -0.1875 to 0.1875
Outputs:
- layer_out: bfloat16 [4, 16384, 1024], P('dp', 'seq')
- grad_input: bfloat16 [4, 16384, 1024], P('dp', 'seq')
- grad_gate_up: float32 [1024, 2048], P(('dp', 'seq'))
- grad_down: float32 [1024, 1024], P(('dp', 'seq'))
- grad_fine: float32 [8, 128, 128], replicated
- grad_coarse: float32 [8, 128, 128], replicated
- grad_gain_mix: float32 [1024], replicated
- grad_gain_mlp: float32 [1024], replicated
The draws below stay inside these ranges and needn't reach their ends.
Inputs may be any that keep to these rules, and one draw needn't show every extreme that they name: `fine_factor`: each group's factor is lower triangular: entries above the diagonal are zero. `coarse_factor`: each group's factor is lower triangular: entries above the diagonal are zero.
All inputs are finite; a program needn't handle non-finite values.
Results may differ from the reference program's by a relative error of at most 0.012.
Values may be sent and summed in bfloat16 or wider, within the bound.
No kernel may reach another device: no remote copies, remote signals or barrier semaphores. Data moves between devices by JAX's collectives and lax.ppermute only.
A program may use at most 192 MiB of HBM per device.

```python
import math
import jax
import jax.numpy as jnp
from jax import lax

D = 1024
FF = 1024
NB = 128
NC = 128
GW = 128
G = 8
LEN = 16384
SEQS = 4


def factor_draw(key, groups, order):
    entries_raw = jnp.clip(jax.random.normal(key, (groups, order, order), jnp.float32), -4.0, 4.0)
    row_index = lax.broadcasted_iota(jnp.int32, (groups, order, order), 1)
    col_index = lax.broadcasted_iota(jnp.int32, (groups, order, order), 2)
    lower_part = 0.8 * entries_raw * lax.rsqrt(row_index.astype(jnp.float32) + 1.0)
    diagonal_part = 1.0 + 0.2 * jnp.tanh(entries_raw)
    factor_values = jnp.where(col_index < row_index, lower_part, jnp.where(col_index == row_index, diagonal_part, 0.0))
    return factor_values.astype(jnp.bfloat16)


def draw_fine_factor(key, part):
    return factor_draw(jax.random.fold_in(key, 3), G, NB)


def draw_coarse_factor(key, part):
    return factor_draw(jax.random.fold_in(key, 7), G, NC)


def spiked(array, rng, source, target, shards_of, factor):
    owner, partner = [(jnp.arange(array.shape[dim]) // (array.shape[dim] // shards_of)).reshape([-1 if axis == dim else 1 for axis in range(array.ndim)]) for dim in (source, target)]
    chosen = jax.random.permutation(rng, shards_of)[partner]
    strong = (owner == chosen) | (owner == (partner + shards_of // 2) % shards_of)
    return jnp.where(strong, factor * array, array)


def levels(own_key, shape, cuts, low, high):
    def one(axis_at, shards_of):
        draws = jax.random.uniform(jax.random.fold_in(jax.random.fold_in(own_key, 6), axis_at), (shards_of,), jnp.float32, low / len(cuts), high / len(cuts))
        return jnp.repeat(jnp.exp(draws), shape[axis_at] // shards_of).reshape((-1,) + (1,) * (len(shape) - axis_at - 1))

    loudness = one(*cuts[0])
    for cut in cuts[1:]:
        loudness = loudness * one(*cut)
    return loudness


def scatter_about(rng, extent, spread, bound, split=(), kind=jnp.bfloat16):
    loudness = levels(rng, extent, split, -0.22, 0.18) if split else 1.0
    values = jax.random.normal(rng, extent, jnp.float32) * spread * loudness
    return jnp.minimum(jnp.maximum(values, -bound), bound).astype(kind)


def heavy_noise(stream_key, extent, deviation, most, pieces, heavy, held_as=jnp.bfloat16):
    result = deviation * jax.random.normal(stream_key, extent, jnp.float32)
    if pieces:
        result = result * levels(stream_key, extent, pieces, -0.22, 0.18)
    return jnp.clip(spiked(result, jax.random.fold_in(stream_key, 3), *heavy), -most, most).astype(held_as)


def setup_inputs(seed: int = 0) -> dict:
    splits = jax.random.split(jax.random.key(seed), 9)
    tokens = heavy_noise(splits[0], (SEQS, LEN, D), 1.0, 6.0, ((0, 4), (1, 8)), (1, 2, 8, 2.0))
    cotangent = scatter_about(splits[1], (SEQS, LEN, D), 1.0, 6.0, ((0, 4), (1, 8)))
    gain_mix = jnp.clip(1.0 + 0.15 * jax.random.normal(splits[2], (D,), jnp.float32), 0.25, 1.75)
    gain_mlp = jnp.clip(1.0 + 0.15 * jax.random.normal(splits[3], (D,), jnp.float32), 0.25, 1.75)
    fine_factor = draw_fine_factor(jax.random.fold_in(splits[8], 71), 0)
    coarse_factor = draw_coarse_factor(jax.random.fold_in(splits[8], 71), 0)
    w_gate_up = scatter_about(splits[6], (D, 2 * FF), D ** -0.5, 0.1875, ((0, 32),))
    w_down = scatter_about(splits[7], (D, FF), FF ** -0.5, 0.1875, ((0, 32),))
    return {"tokens": tokens, "cotangent": cotangent, "gain_mix": gain_mix, "gain_mlp": gain_mlp, "fine_factor": fine_factor, "coarse_factor": coarse_factor, "w_gate_up": w_gate_up, "w_down": w_down}


epsilon = 1e-05

def widen(values):
    return lax.optimization_barrier(values.astype(jnp.bfloat16)).astype(jnp.float32)

def norm_rows(values):
    scale_inv = lax.rsqrt(lax.optimization_barrier(jnp.mean(values * values, axis=-1, keepdims=True)) + epsilon)
    return (values * scale_inv, scale_inv)

def norm_back(upstream, normed, scale_inv):
    return scale_inv * (upstream - normed * lax.optimization_barrier(jnp.mean(upstream * normed, axis=-1, keepdims=True)))

def silu_parts(gate_pre):
    squash = jax.nn.sigmoid(gate_pre)
    return (gate_pre * squash, squash * (1.0 + gate_pre * (1.0 - squash)))

def reference(tokens, cotangent, gain_mix, gain_mlp, fine_factor, coarse_factor, w_gate_up, w_down):
    fine_weights = fine_factor.astype(jnp.float32)
    coarse_weights = coarse_factor.astype(jnp.float32)

    def one_sequence(totals, sequence_pair):
        inputs, upstream_out = sequence_pair
        source = inputs.astype(jnp.float32)
        normed_mix, inv_mix = norm_rows(source)
        gated_in = widen(normed_mix * gain_mix)
        blocked = gated_in.reshape(NC, NB, G, GW)
        fine_mixed = widen(jnp.einsum('gpq,aqgc->apgc', fine_weights, blocked))
        coarse_mixed = widen(jnp.einsum('gpq,qbgc->pbgc', coarse_weights, fine_mixed))
        mixed = coarse_mixed.reshape(LEN, D)
        after_mix = source + mixed * gated_in
        normed_mlp, inv_mlp = norm_rows(after_mix)
        mlp_in = (normed_mlp * gain_mlp).astype(jnp.bfloat16)
        both = jnp.dot(mlp_in, w_gate_up, preferred_element_type=jnp.float32)
        gate_pre = both[:, :FF]
        upward = both[:, FF:]
        silu_gate, silu_slope = silu_parts(gate_pre)
        activation = (silu_gate * upward).astype(jnp.bfloat16)
        layer = (after_mix + jnp.dot(activation, w_down.T, preferred_element_type=jnp.float32)).astype(jnp.bfloat16)
        upstream = upstream_out.astype(jnp.float32)
        back_act = widen(jnp.dot(upstream_out, w_down, preferred_element_type=jnp.float32))
        back_both = jnp.concatenate([back_act * upward * silu_slope, back_act * silu_gate], axis=1).astype(jnp.bfloat16)
        back_mlp_in = jnp.dot(back_both, w_gate_up.T, preferred_element_type=jnp.float32)
        gain_mlp_term = lax.optimization_barrier(jnp.sum(back_mlp_in * normed_mlp, axis=0))
        back_after = upstream + norm_back(back_mlp_in * gain_mlp, normed_mlp, inv_mlp)
        back_mixed = widen(back_after * gated_in).reshape(NC, NB, G, GW)
        back_fine = widen(jnp.einsum('gpq,pbgc->qbgc', coarse_weights, back_mixed))
        coarse_term = jnp.einsum('pbgc,qbgc->gpq', back_mixed, fine_mixed)
        back_blocked = jnp.einsum('gpq,apgc->aqgc', fine_weights, back_fine).reshape(LEN, D)
        fine_term = jnp.einsum('apgc,aqgc->gpq', back_fine, blocked)
        back_hidden = back_after * mixed + back_blocked
        gain_mix_term = lax.optimization_barrier(jnp.sum(back_hidden * normed_mix, axis=0))
        grad_in = (back_after + norm_back(back_hidden * gain_mix, normed_mix, inv_mix)).astype(jnp.bfloat16)
        gate_up_term = jnp.dot(mlp_in.T, back_both, preferred_element_type=jnp.float32)
        down_term = jnp.dot(upstream_out.T, activation, preferred_element_type=jnp.float32)
        new_totals = (totals[0] + gate_up_term, totals[1] + down_term, totals[2] + fine_term, totals[3] + coarse_term, totals[4] + gain_mix_term, totals[5] + gain_mlp_term)
        return (new_totals, (layer, grad_in))
    start_totals = (jnp.zeros((D, 2 * FF), jnp.float32), jnp.zeros((D, FF), jnp.float32), jnp.zeros((G, NB, NB), jnp.float32), jnp.zeros((G, NC, NC), jnp.float32), jnp.zeros((D,), jnp.float32), jnp.zeros((D,), jnp.float32))
    final_totals, stacked = lax.scan(one_sequence, start_totals, (tokens, cotangent))
    scale_tokens = 1.0 / math.sqrt(SEQS * LEN)
    grad_fine = jnp.tril(final_totals[2]) * (1.0 / math.sqrt(SEQS * NC * GW))
    grad_coarse = jnp.tril(final_totals[3]) * (1.0 / math.sqrt(SEQS * NB * GW))
    return (stacked[0], stacked[1], final_totals[0] * scale_tokens, final_totals[1] * scale_tokens, grad_fine, grad_coarse, final_totals[4] * scale_tokens, final_totals[5] * scale_tokens)
```

```python
import functools
import math

import jax
import jax.numpy as jnp
from jax import lax
from jax.experimental import pallas as pl
from jax.experimental.pallas import tpu as pltpu
from jax.sharding import PartitionSpec as P

D = 1024
FF = 1024
NB = 128
NC = 128
GW = 128
G = D // GW
HG = G // 2
HALF = D // 2
STRIP = 256

epsilon = 1e-05
F32 = jnp.float32
BF16 = jnp.bfloat16
NT = (((1,), (1,)), ((), ()))
MIB = 1 << 20


def dot(left, right):
    return jnp.dot(left, right, preferred_element_type=F32)


def dot_nt(left, right):
    return lax.dot_general(left, right, NT, preferred_element_type=F32)


def inv_rms(values):
    return lax.rsqrt(jnp.mean(values * values, axis=-1, keepdims=True) + epsilon)


def params(mib):
    return pltpu.CompilerParams(vmem_limit_bytes=mib * MIB)


def cost():
    return pl.CostEstimate(flops=1, bytes_accessed=1, transcendentals=0)


class Order:
    before = []

    @classmethod
    def mark(cls, *values):
        cls.before = list(values)

    @classmethod
    def also(cls, *values):
        cls.before = cls.before + list(values)


def run(kernel, in_specs, operands, **rest):
    extra = Order.before
    count = len(operands)

    def body(*refs):
        kernel(*refs[:count], *refs[count + len(extra):])

    outs = pl.pallas_call(
        body,
        in_specs=list(in_specs) + [pl.BlockSpec(memory_space=pl.ANY)] * len(extra),
        cost_estimate=cost(),
        **rest,
    )(*operands, *extra)
    Order.mark(outs[-1] if isinstance(outs, (list, tuple)) else outs)
    return outs


def lanes_of(blocks, group):
    part = slice(group * GW, (group + 1) * GW)
    return jnp.concatenate([blocks[i, :, part] for i in range(blocks.shape[0])], axis=1)


def spread(rows, plane, own, other, count, width):
    for slot, out in enumerate((own, other)):
        half = plane if slot == 0 else 1 - plane
        for local in range(HG):
            for b in range(width):
                at = (local * width + b) * GW
                took = rows[half * HG + local, pl.ds(b, count, stride=width), :]
                out[:, at:at + GW] = took.astype(BF16)


def collect(rows, plane, own, other, count, width):
    for slot, part in enumerate((own, other)):
        half = plane if slot == 0 else 1 - plane
        for local in range(HG):
            for b in range(width):
                at = (local * width + b) * GW
                took = part[:, at:at + GW].astype(F32)
                rows[half * HG + local, pl.ds(b, count, stride=width), :] = took
    return jnp.concatenate([rows[group] for group in range(G)], axis=1)


def fine_kernel(unit, starts, plane, tok, gain, factor, *refs):
    outs, hidden, rows = refs[:-2], refs[-2], refs[-1]
    count = tok.shape[0]
    low = min(starts)
    span = rows.shape[0] // count
    high = low + span
    for i in range(count):
        source = tok[i].astype(F32)
        hidden[i] = (source * inv_rms(source) * gain[...]).astype(BF16)
    for slot in range(2):
        half = plane[0] if slot == 0 else 1 - plane[0]
        for local in range(HG):
            group = half * HG + local
            lanes = pl.ds(pl.multiple_of(group * GW, GW), GW)
            side = jnp.concatenate([hidden[i, :, lanes] for i in range(count)], axis=1)
            mixed = dot(factor[group, low:high], side)
            for i in range(count):
                rows[i * span:(i + 1) * span, :] = mixed[:, i * GW:(i + 1) * GW]
            for chunk, start in enumerate(starts):
                out = outs[chunk] if slot == 0 else outs[-1]
                units = outs[chunk].shape[1] // (HG * unit * GW)
                skip = chunk * units if slot == 1 else 0
                start -= low
                for u in range(units):
                    for b in range(unit):
                        at = (((skip + u) * HG + local) * unit + b) * GW
                        took = rows[pl.ds(start + u * unit + b, count, stride=span), :]
                        out[:, at:at + GW] = took.astype(BF16)


def fine_forward(plane, tokens, gain, factor, starts, widths, unit):
    blocks = tokens.shape[0]
    shapes = [(blocks, width * HALF) for width in widths]
    shapes.append((blocks, sum(widths) * HALF))
    full = lambda shape: pl.BlockSpec(shape, lambda i: (0,) * len(shape))
    return run(
        functools.partial(fine_kernel, unit, starts),
        grid=(1,),
        in_specs=[
            pl.BlockSpec(memory_space=pltpu.SMEM),
            full((blocks, NB, D)),
            full((1, D)),
            full((G, NB, NB)),
        ],
        out_specs=[full(shape) for shape in shapes],
        out_shape=[jax.ShapeDtypeStruct(shape, BF16) for shape in shapes],
        scratch_shapes=[pltpu.VMEM((blocks, NB, D), BF16), pltpu.VMEM((blocks * sum(widths), GW), F32)],
        compiler_params=params(48),
        operands=[plane, tokens, gain, factor],
        name="fine_forward",
    )


def join_kernel(plane, own, other, out, rows):
    count, width = out.shape[:2]
    out[...] = collect(rows, plane[0], own, other, count, width).astype(BF16).reshape(out.shape)


def join(plane, own, other, unit):
    blocks, lanes = own.shape
    width = lanes // HALF
    half = pl.BlockSpec((blocks, unit * HALF), lambda i: (0, i))
    return run(
        join_kernel,
        grid=(width // unit,),
        in_specs=[pl.BlockSpec(memory_space=pltpu.SMEM), half, half],
        out_specs=pl.BlockSpec((blocks, unit, D), lambda i: (0, i, 0)),
        out_shape=jax.ShapeDtypeStruct((blocks, width, D), BF16),
        scratch_shapes=[pltpu.VMEM((G, blocks * unit, GW), F32)],
        compiler_params=params(24),
        operands=[plane, own, other],
        name="join",
    )


def coarse_kernel(count, *refs):
    weight, base, part = refs[count:]
    stacked = jnp.concatenate([raw[...] for raw in refs[:count]], axis=0)
    high = base.shape[0]
    lanes = base.shape[1] // HG
    for group in range(HG):
        strip = slice(group * lanes, (group + 1) * lanes)
        total = dot(weight[group], stacked[:, strip]).astype(BF16)
        base[:, strip] = total[:high]
        part[:, strip] = total[high:]


def coarse_mix(raws, weight, unit):
    lanes = raws[0].shape[1]
    tile = unit * HALF
    out_rows = weight.shape[1] // 2
    half = pl.BlockSpec((out_rows, tile), lambda t: (0, t))
    return run(
        functools.partial(coarse_kernel, len(raws)),
        grid=(lanes // tile,),
        in_specs=[
            *[pl.BlockSpec((raw.shape[0], tile), lambda t: (0, t)) for raw in raws],
            pl.BlockSpec(weight.shape, lambda t: (0, 0, 0)),
        ],
        out_specs=[half, half],
        out_shape=[jax.ShapeDtypeStruct((out_rows, lanes), BF16)] * 2,
        compiler_params=params(32),
        operands=[*raws, weight],
        name="coarse_mix",
    )


def stack_kernel(own, other, out):
    count = own.shape[0]
    out[:count] = own[...]
    out[count:] = other[...]


def stack(own, other, unit, at=0):
    blocks, lanes = own.shape
    tile = unit * HALF
    skip = at * lanes // tile
    half = pl.BlockSpec((blocks, tile), lambda t: (0, t))
    taken = pl.BlockSpec((blocks, tile), lambda t: (0, skip + t))
    return run(
        stack_kernel,
        grid=(lanes // tile,),
        in_specs=[half, taken],
        out_specs=pl.BlockSpec((2 * blocks, tile), lambda t: (0, t)),
        out_shape=jax.ShapeDtypeStruct((2 * blocks, lanes), BF16),
        compiler_params=params(16),
        operands=[own, other],
        name="stack",
    )


def add_kernel(flag, base, extra, own, other):
    count = own.shape[0]
    more = jnp.where(flag[0] == 1, extra[...].astype(F32), 0.0)
    total = (base[...].astype(F32) + more).astype(BF16)
    own[...] = total[:count]
    other[...] = total[count:]


def add_split(flag, base, extra, unit):
    blocks, lanes = base.shape[0] // 2, base.shape[1]
    tile = unit * HALF
    whole = pl.BlockSpec((2 * blocks, tile), lambda t: (0, t))
    half = pl.BlockSpec((blocks, tile), lambda t: (0, t))
    return run(
        add_kernel,
        grid=(lanes // tile,),
        in_specs=[pl.BlockSpec(memory_space=pltpu.SMEM), whole, whole],
        out_specs=[half, half],
        out_shape=[jax.ShapeDtypeStruct((blocks, lanes), BF16)] * 2,
        compiler_params=params(16),
        operands=[flag, base, extra],
        name="add_split",
    )


def coarse_grad_kernel(ups, downs, *refs):
    upper = jnp.concatenate([ref[...] for ref in refs[:ups]], axis=0)
    lower = jnp.concatenate([ref[...] for ref in refs[ups:ups + downs]], axis=0)
    out = refs[-1]
    lanes = upper.shape[1] // HG

    @pl.when(pl.program_id(0) == 0)
    def _():
        out[...] = jnp.zeros_like(out)

    for group in range(HG):
        strip = slice(group * lanes, (group + 1) * lanes)
        out[group] += dot_nt(upper[:, strip], lower[:, strip])


def coarse_grad(uppers, lowers, unit):
    lanes = uppers[0].shape[1]
    tile = unit * HALF
    high = sum(u.shape[0] for u in uppers)
    wide = sum(v.shape[0] for v in lowers)
    return run(
        functools.partial(coarse_grad_kernel, len(uppers), len(lowers)),
        grid=(lanes // tile,),
        in_specs=[pl.BlockSpec((v.shape[0], tile), lambda t: (0, t)) for v in uppers + lowers],
        out_specs=pl.BlockSpec((HG, high, wide), lambda t: (0, 0, 0)),
        out_shape=jax.ShapeDtypeStruct((HG, high, wide), F32),
        compiler_params=params(32),
        operands=[*uppers, *lowers],
        name="coarse_grad",
    )


def mlp_kernel(plane, tok, cot, own, other, gain_mix, gain_mlp, weights, *refs):
    layer, mlp_in, active, back_both, back_after, mixed, back_own, back_other = refs[-10:-2]
    gain_sum, rows = refs[-2:]
    shape = tok.shape
    flat = (shape[0] * shape[1], D)
    taken = collect(rows, plane[0], own, other, shape[0], shape[1])
    mixed[...] = taken.astype(BF16).reshape(shape)
    source = tok[...].reshape(flat).astype(F32)
    hidden = (source * inv_rms(source) * gain_mix[...]).astype(BF16).astype(F32)
    after = source + taken * hidden
    scale = inv_rms(after)
    normed = after * scale
    entering = (normed * gain_mlp[...]).astype(BF16)
    mlp_in[...] = entering.reshape(shape)
    upstream = cot[...].reshape(flat)
    active_parts, gate_parts, up_parts = [], [], []
    for start in range(0, FF, STRIP):
        strip = slice(start, start + STRIP)
        gate = dot(entering, weights[:, strip])
        upward = dot(entering, weights[:, FF + start:FF + start + STRIP])
        back_act = dot(upstream, weights[:, 2 * FF + start:2 * FF + start + STRIP])
        back_act = back_act.astype(BF16).astype(F32)
        squash = jax.nn.sigmoid(gate)
        silu = gate * squash
        slope = squash * (1.0 + gate * (1.0 - squash))
        active_parts.append((silu * upward).astype(BF16))
        gate_parts.append((back_act * upward * slope).astype(BF16))
        up_parts.append((back_act * silu).astype(BF16))
    activation = jnp.concatenate(active_parts, axis=1)
    back_gate = jnp.concatenate(gate_parts, axis=1)
    back_up = jnp.concatenate(up_parts, axis=1)
    active[...] = activation.reshape(shape)
    back_both[:, :, :FF] = back_gate.reshape(shape)
    back_both[:, :, FF:] = back_up.reshape(shape)
    layer[...] = (after + dot_nt(activation, weights[:, 2 * FF:])).astype(BF16).reshape(shape)
    back_in = dot_nt(back_gate, weights[:, :FF]) + dot_nt(back_up, weights[:, FF:2 * FF])

    @pl.when(pl.program_id(0) == 0)
    def _():
        gain_sum[...] = jnp.zeros_like(gain_sum)

    gain_sum[...] += jnp.sum(back_in * normed, axis=0, keepdims=True)
    weighted = back_in * gain_mlp[...]
    centre = jnp.mean(weighted * normed, axis=-1, keepdims=True)
    total = upstream.astype(F32) + scale * (weighted - normed * centre)
    back_after[...] = total.astype(BF16).reshape(shape)
    back_mixed = total * hidden
    for group in range(G):
        rows[group] = back_mixed[:, group * GW:(group + 1) * GW]
    spread(rows, plane[0], back_own, back_other, shape[0], shape[1])


def mlp(plane, tokens, cotangent, own, other, gain_mix, gain_mlp, weights, kept, start, unit):
    blocks, lanes = own.shape
    width = lanes // HALF
    first = start // unit
    whole = pl.BlockSpec((blocks, unit, D), lambda i: (0, first + i, 0))
    local = pl.BlockSpec((blocks, unit, D), lambda i: (0, i, 0))
    half = pl.BlockSpec((blocks, unit * HALF), lambda i: (0, i))
    gain = pl.BlockSpec((1, D), lambda i: (0, 0))
    operands = [plane, tokens, cotangent, own, other, gain_mix, gain_mlp, weights]
    specs = [pl.BlockSpec(memory_space=pltpu.SMEM), whole, whole, half, half, gain, gain]
    specs.append(pl.BlockSpec((D, 3 * FF), lambda i: (0, 0)))
    aliases = {len(operands) + i: i for i in range(len(kept))}
    operands += kept
    specs += [pl.BlockSpec(memory_space=pl.ANY)] * len(kept)
    part = jax.ShapeDtypeStruct((blocks, width, D), BF16)
    full = jax.ShapeDtypeStruct((blocks, NB, D), BF16)
    return run(
        mlp_kernel,
        grid=(width // unit,),
        in_specs=specs,
        out_specs=[
            whole,
            whole,
            whole,
            pl.BlockSpec((blocks, unit, 2 * FF), lambda i: (0, first + i, 0)),
            local,
            local,
            half,
            half,
            gain,
        ],
        out_shape=[
            full,
            full,
            full,
            jax.ShapeDtypeStruct((blocks, NB, 2 * FF), BF16),
            part,
            part,
            jax.ShapeDtypeStruct((blocks, lanes), BF16),
            jax.ShapeDtypeStruct((blocks, lanes), BF16),
            jax.ShapeDtypeStruct((1, D), F32),
        ],
        scratch_shapes=[pltpu.VMEM((G, blocks * unit, GW), F32)],
        input_output_aliases=aliases,
        compiler_params=params(56),
        operands=operands,
        name="mlp",
    )


def weight_kernel(has_prior, mlp_in, active, back_both, cot, *refs):
    outs, total = refs[-3:-1], refs[-1]
    count = mlp_in.shape[0] * mlp_in.shape[1]
    step, steps = pl.program_id(0), pl.num_programs(0)
    turn = (((0,), (0,)), ((), ()))
    entering = mlp_in[...].reshape(count, D)
    upstream = cot[...].reshape(count, D)

    @pl.when(step == 0)
    def _():
        total[...] = jnp.zeros_like(total)

    for start in range(0, 3 * FF, STRIP):
        if start < 2 * FF:
            left, right = entering, back_both[:, :, start:start + STRIP]
        else:
            left, right = upstream, active[:, :, start - 2 * FF:start - 2 * FF + STRIP]
        total[:, start:start + STRIP] += lax.dot_general(
            left, right.reshape(count, STRIP), turn, preferred_element_type=F32
        )

    @pl.when(step == steps - 1)
    def _():
        for i, out in enumerate(outs):
            wide = out.shape[1]
            result = total[:, i * wide:(i + 1) * wide]
            if has_prior:
                result = result + refs[i][...].astype(F32)
            out[...] = result.astype(BF16)


def weight_grads_of(kept, cotangent, prior, low, high, unit):
    blocks = cotangent.shape[0]
    first = low // unit
    block = pl.BlockSpec((blocks, unit, D), lambda k: (0, first + k, 0))
    wide = pl.BlockSpec((blocks, unit, 2 * FF), lambda k: (0, first + k, 0))
    half = pl.BlockSpec((D, 3 * FF // 2), lambda k: (0, 0))
    return run(
        functools.partial(weight_kernel, bool(prior)),
        grid=((high - low) // unit,),
        in_specs=[block, block, wide, block] + [half] * len(prior),
        out_specs=[half, half],
        out_shape=[jax.ShapeDtypeStruct((D, 3 * FF // 2), BF16)] * 2,
        scratch_shapes=[pltpu.VMEM((D, 3 * FF), F32)],
        compiler_params=params(56),
        operands=[kept[1], kept[2], kept[3], cotangent, *prior],
        name="weight_grad",
    )


def finish(source, gain, back_after, mixed, blocked):
    scale = inv_rms(source)
    normed = source * scale
    back_hidden = back_after * mixed + blocked
    weighted = back_hidden * gain
    centre = jnp.mean(weighted * normed, axis=-1, keepdims=True)
    return back_hidden * normed, back_after + scale * (weighted - normed * centre)


def tail_kernel(count, unit, tok, gain, factor, *refs):
    backs, mixes, fines = (refs[i * count:(i + 1) * count] for i in range(3))
    grad, rest, fine_term, gain_sum, blocked = refs[3 * count:]
    steps = tok.shape[0]

    @pl.when(pl.program_id(0) == 0)
    def _():
        fine_term[...] = jnp.zeros_like(fine_term)
        gain_sum[...] = jnp.zeros_like(gain_sum)

    source = tok[...].astype(F32)
    hidden = (source * inv_rms(source) * gain[...]).astype(BF16)
    back_fine = jnp.concatenate([ref[...] for ref in fines], axis=1)
    for group in range(G):
        upper = lanes_of(back_fine, group)
        result = dot(factor[group], upper)
        for i in range(steps):
            blocked[i, :, group * GW:(group + 1) * GW] = result[:, i * GW:(i + 1) * GW]
        fine_term[group] += dot_nt(upper, lanes_of(hidden, group))
    back_after = jnp.concatenate([ref[...] for ref in backs], axis=1).astype(F32)
    mixed = jnp.concatenate([ref[...] for ref in mixes], axis=1).astype(F32)
    terms, grads = finish(source[:, unit:], gain[...], back_after, mixed, blocked[:, unit:])
    gain_sum[...] += jnp.sum(jnp.sum(terms, axis=0), axis=0, keepdims=True)
    grad[:, unit:] = grads.astype(BF16)
    grad[:, :unit] = jnp.zeros_like(grad[:, :unit])
    rest[...] = blocked[:, :unit]


def tail(tokens, gain, factor, backs, mixes, fines, unit):
    blocks = tokens.shape[0]
    step = min(2, blocks)
    one = pl.BlockSpec((step, NB, D), lambda i: (i, 0, 0))

    def rows(arrays):
        return [pl.BlockSpec((step, v.shape[1], D), lambda i: (i, 0, 0)) for v in arrays]

    return run(
        functools.partial(tail_kernel, len(backs), unit),
        grid=(blocks // step,),
        in_specs=[
            one,
            pl.BlockSpec((1, D), lambda i: (0, 0)),
            pl.BlockSpec(factor.shape, lambda i: (0, 0, 0)),
            *rows(backs),
            *rows(mixes),
            *rows(fines),
        ],
        out_specs=[
            one,
            pl.BlockSpec((step, unit, D), lambda i: (i, 0, 0)),
            pl.BlockSpec((G, NB - unit, NB), lambda i: (0, 0, 0)),
            pl.BlockSpec((1, D), lambda i: (0, 0)),
        ],
        out_shape=[
            jax.ShapeDtypeStruct((blocks, NB, D), BF16),
            jax.ShapeDtypeStruct((blocks, unit, D), F32),
            jax.ShapeDtypeStruct((G, NB - unit, NB), F32),
            jax.ShapeDtypeStruct((1, D), F32),
        ],
        scratch_shapes=[pltpu.VMEM((step, NB, D), F32)],
        compiler_params=params(48),
        operands=[tokens, gain, factor, *backs, *mixes, *fines],
        name="fine_backward",
    )


def last_kernel(tok, gain, factor, back, mix, fine, rest, _, grad, fine_term, gain_sum, blocked):
    blocks = tok.shape[0]
    source = tok[...].astype(F32)
    hidden = (source * inv_rms(source) * gain[...]).astype(BF16)
    back_fine = fine[...]
    for group in range(G):
        upper = lanes_of(back_fine, group)
        result = dot(factor[group], upper)
        for i in range(blocks):
            part = slice(group * GW, (group + 1) * GW)
            blocked[i, :, part] = rest[i, :, part] + result[:, i * GW:(i + 1) * GW]
        fine_term[group] = dot_nt(upper, lanes_of(hidden, group))
    terms, grads = finish(source, gain[...], back[...].astype(F32), mix[...].astype(F32), blocked[...])
    gain_sum[...] = jnp.sum(jnp.sum(terms, axis=0), axis=0, keepdims=True)
    grad[...] = grads.astype(BF16)


def last(tokens, gain, factor, back, mix, fine, rest, grad):
    blocks, unit = back.shape[:2]
    one = pl.BlockSpec((blocks, unit, D), lambda i: (0, 0, 0))
    return run(
        last_kernel,
        grid=(1,),
        in_specs=[
            one,
            pl.BlockSpec((1, D), lambda i: (0, 0)),
            pl.BlockSpec(factor.shape, lambda i: (0, 0, 0)),
            one,
            one,
            one,
            one,
            pl.BlockSpec(memory_space=pl.ANY),
        ],
        out_specs=[
            one,
            pl.BlockSpec((G, unit, unit), lambda i: (0, 0, 0)),
            pl.BlockSpec((1, D), lambda i: (0, 0)),
        ],
        out_shape=[
            jax.ShapeDtypeStruct(grad.shape, BF16),
            jax.ShapeDtypeStruct((G, unit, unit), F32),
            jax.ShapeDtypeStruct((1, D), F32),
        ],
        input_output_aliases={7: 0},
        scratch_shapes=[pltpu.VMEM((blocks, unit, D), F32)],
        compiler_params=params(48),
        operands=[tokens, gain, factor, back, mix, fine, rest, grad],
        name="fine_backward_last",
    )


def reduce_all(value, axes, first=1):
    for axis in axes:
        size = lax.axis_size(axis)
        reach = first
        while reach < size:
            pairs = [(i, i ^ reach) for i in range(size)]
            value = value + lax.ppermute(value, axis, pairs)
            reach *= 2
    return value


def split_kernel(inner, has_arrived, bit, value, *refs):
    keep, away = refs[-2:]
    side = bit[0]
    for j in range(keep.shape[0]):
        base = j // inner * 2 * inner + j % inner
        mine, theirs = base + side * inner, base + (1 - side) * inner
        if has_arrived:
            keep[j] = value[mine] + refs[0][mine]
            away[j] = value[theirs] + refs[0][theirs]
        else:
            keep[j] = value[mine]
            away[j] = value[theirs]


def split(bit, value, arrived, inner):
    shape = (value.shape[0] // 2,) + value.shape[1:]
    full = lambda shape: pl.BlockSpec(shape, lambda i: (0,) * len(shape))
    more = [] if arrived is None else [arrived]
    return run(
        functools.partial(split_kernel, inner, bool(more)),
        grid=(1,),
        in_specs=[pl.BlockSpec(memory_space=pltpu.SMEM)] + [full(value.shape)] * (1 + len(more)),
        out_specs=[full(shape)] * 2,
        out_shape=[jax.ShapeDtypeStruct(shape, BF16)] * 2,
        compiler_params=params(32),
        operands=[bit, value, *more],
        name="split",
    )


class Scatter:

    def __init__(self, value, late):
        bits = []
        for axis in ("dp", "seq"):
            size = lax.axis_size(axis)
            bits += [(axis, 1 << k) for k in reversed(range(size.bit_length() - 1))]
        outer = [bit for bit in reversed(bits) if bit[0] == "dp"]
        inner = [bit for bit in reversed(bits) if bit[0] == "seq"]
        self.order = outer[:1] + inner[:1] + outer[1:] + inner[1:] if late else outer + inner
        self.left = bits
        self.columns = value.shape[1]
        self.value = value.reshape(2 ** len(bits), -1, self.columns)
        self.arriving = None

    def step(self):
        if not self.order:
            self.value, self.arriving = self.value + self.arriving, None
            return
        axis, reach = self.order.pop(0)
        at = self.left.index((axis, reach))
        self.left = self.left[:at] + self.left[at + 1:]
        inner = 2 ** (len(self.left) - at)
        size = lax.axis_size(axis)
        bit = ((lax.axis_index(axis) // reach) % 2).astype(jnp.int32).reshape(1)
        self.value, away = split(bit, self.value, self.arriving, inner)
        self.arriving = lax.ppermute(away, axis, [(i, i ^ reach) for i in range(size)])


def gather_rows(value):
    steps = []
    for axis in ("seq", "dp"):
        size = lax.axis_size(axis)
        reaches = [1 << k for k in range(size.bit_length() - 1)]
        steps += [(axis, reach) for reach in reversed(reaches)]
    rows, columns = value.shape
    value = value[None]
    for axis, reach in steps:
        pairs = [(i, i ^ reach) for i in range(lax.axis_size(axis))]
        other = lax.ppermute(value, axis, pairs)
        low = lax.axis_index(axis) // reach % 2 == 0
        value = jnp.concatenate(
            [jnp.where(low, value, other), jnp.where(low, other, value)], axis=0
        )
    count = len(steps)
    stepped = list(reversed(steps))
    wanted = [(axis, 1 << k) for axis in ("dp", "seq")
              for k in reversed(range(lax.axis_size(axis).bit_length() - 1))]
    value = value.reshape((2,) * count + (rows, columns))
    order = [stepped.index(bit) for bit in wanted]
    return value.transpose(*order, count, count + 1).reshape(-1, columns)


def on_device(tokens, cotangent, gain_mix, gain_mlp, fine_factor, coarse_factor, w_gate_up, w_down):
    rows = tokens.shape[1]
    blocks = rows // NB
    seq_devices = lax.axis_size("seq")
    data_devices = lax.axis_size("dp")
    planes = 2
    depth = seq_devices // planes
    index = lax.axis_index("seq")
    level, plane = index // planes, index % planes
    unit = max(16, 256 // blocks)
    width = min(2 * unit, NB // 2)
    widths = [width] * (NB // width)

    def shift(value, by, low=0, high=None):
        top = depth - 1 if high is None else high
        pairs = [
            (lv * planes + p, (lv + by) * planes + p)
            for lv in range(depth)
            for p in range(planes)
            if low <= lv + by <= top
        ]
        return lax.ppermute(value, "seq", pairs)

    def swap(value):
        return lax.ppermute(value, "seq", [(i, i ^ 1) for i in range(seq_devices)])

    weights = gather_rows(jnp.concatenate([w_gate_up, w_down], axis=1))
    token_blocks = tokens.reshape(blocks, NB, D)
    cot_blocks = cotangent.reshape(blocks, NB, D)
    row_mix, row_mlp = gain_mix.reshape(1, D), gain_mlp.reshape(1, D)

    pair = planes * blocks
    local = jnp.arange(pair)
    order = jnp.where(plane == 0, local, (local + blocks) % pair)

    def picks(*levels):
        wanted = jnp.concatenate([order + lv * pair for lv in levels])
        return (wanted[:, None] == jnp.arange(NC)[None, :]).astype(BF16)

    reaches = list(range(max(2, depth - 1)))
    far = reaches[-1]
    up_levels = [level - d for d in reaches[:-1]] + [jnp.where(level == far, 0, depth)]
    down_levels = [level + d for d in reaches[:-1]] + [jnp.where(level == 1, depth - 1, depth)]
    rows_up, columns_up = picks(level, level + 1), picks(*up_levels)
    rows_down, columns_down = picks(level, level - 1), picks(*down_levels)
    spot = (jnp.arange(2 * pair)[:, None] >= pair) & (jnp.arange(len(reaches) * pair)[None] < pair)
    factor = lax.dynamic_slice_in_dim(coarse_factor, plane * HG, HG, axis=0)

    def chosen(matrix, rows_of, columns_of):
        some = jnp.einsum("rp,gpq->grq", rows_of, matrix, preferred_element_type=F32)
        some = jnp.einsum(
            "grq,cq->grc", some.astype(BF16), columns_of, preferred_element_type=F32
        )
        return jnp.where(spot, 0.0, some).astype(BF16)

    which = plane.reshape(1).astype(jnp.int32)
    count = len(widths)
    starts = [NB - sum(widths[:i + 1]) for i in range(count)]
    steps = range(count)
    state = [dict() for _ in steps]
    kept = []
    sums = {}
    Order.mark()

    def forward(*chunks):
        outs = fine_forward(
            which, token_blocks, row_mix, fine_factor,
            [starts[c] for c in chunks], [widths[c] for c in chunks], unit,
        )
        arrived = swap(outs[-1])
        for at, c in enumerate(chunks):
            state[c]["pair"] = outs[at], arrived, at

    last_flag = (level == depth - 1).astype(jnp.int32).reshape(1)
    first_flag = (level == 0).astype(jnp.int32).reshape(1)

    def jump_up(here, part):
        pairs = []
        for p in range(planes):
            if here is not None:
                pairs.append((p, far * planes + p))
            if part is not None:
                pairs.append((far * planes + p, (depth - 1) * planes + p))
        both = here if part is None else part if here is None else jnp.where(level == 0, here, part)
        return lax.ppermute(both, "seq", pairs)

    def jump_down(here, part):
        pairs = []
        for p in range(planes):
            if here is not None:
                pairs.append(((depth - 1) * planes + p, planes + p))
            if part is not None:
                pairs.append((planes + p, p))
        both = here if part is None else part if here is None else jnp.where(level == 1, part, here)
        return lax.ppermute(both, "seq", pairs)

    def stack_up(c):
        here = part = None
        if c > 0:
            part = state[c - 1]["part"]
        if c < count:
            here = stack(*state[c]["pair"][:2], unit, state[c]["pair"][2])
            middle = [shift(here, d, high=depth - 2) for d in reaches[2:-1]]
            raws = [here, shift(here, 1)] + middle
        leap = jump_up(here, part)
        if c > 0:
            state[c - 1]["extra"] = leap
        if c < count:
            state[c]["raws"] = raws + [leap]

    def mix_up(c):
        state[c]["base"], state[c]["part"] = coarse_mix(state[c]["raws"], up_weight, unit)

    def add_up(c):
        own, other = add_split(last_flag, state[c]["base"], state[c]["extra"], unit)
        state[c]["own"], state[c]["other"] = own, swap(other)

    def run_mlp(c, kept):
        outs = mlp(
            which, token_blocks, cot_blocks, state[c]["own"], state[c]["other"], row_mix, row_mlp,
            weights, kept, starts[c], unit,
        )
        names = ["back_after", "mixed", "down_own", "down_other"]
        state[c].update(zip(names, outs[4:8]))
        sums["gain"] = outs[8] if c == 0 else sums["gain"] + outs[8]
        state[c]["down_other"] = swap(state[c]["down_other"])
        return list(outs[:4])

    def weight_grad(first, end):
        sums["weights"] = weight_grads_of(
            kept, cot_blocks, sums.get("weights", []), starts[end - 1],
            starts[first] + widths[first], unit,
        )

    def stack_down(c):
        here = part = None
        if c > 0:
            part = state[c - 1]["part"]
        if c < count:
            here = stack(state[c]["down_own"], state[c]["down_other"], unit)
            middle = [shift(here, -d, low=1) for d in reaches[2:-1]]
            backs = [here, shift(here, -1)] + middle
        leap = jump_down(here, part)
        if c > 0:
            state[c - 1]["extra"] = leap
        if c < count:
            state[c]["backs"] = backs + [leap]

    def mix_down(c):
        state[c]["base"], state[c]["part"] = coarse_mix(state[c]["backs"], down_weight, unit)

    def add_down(c):
        own, other = add_split(first_flag, state[c]["base"], state[c]["extra"], unit)
        state[c]["fine_own"], state[c]["fine_other"] = own, swap(other)

    def factor_grad(c):
        part = coarse_grad(state[c]["backs"][:2], state[c]["raws"], unit)
        sums["coarse"] = part if c == 0 else sums["coarse"] + part

    def join_down(c):
        state[c]["fine"] = join(which, state[c]["fine_own"], state[c]["fine_other"], unit)

    def scatter_step():
        for part in scatters:
            part.step()

    halfway = count - 1
    up_weight = chosen(factor, rows_up, columns_up)
    down_weight = chosen(factor.transpose(0, 2, 1), rows_down, columns_down)
    forward(0)
    stack_up(0)
    forward(*steps[1:])
    for i in range(count + 1):
        if i < count:
            mix_up(i)
            stack_up(i + 1)
        if i >= 4:
            join_down(i - 4)
        if i >= 1:
            add_up(i - 1)
            if i == count:
                weight_grad(0, halfway)
            kept = run_mlp(i - 1, kept)
        if i >= 2:
            mix_down(i - 2)
        if i >= 1:
            stack_down(i - 1)
        if i == count:
            weight_grad(halfway, count)
            scatters = [Scatter(value, late) for value, late in zip(sums["weights"], (False, True))]
            scatter_step()
        if i >= 2:
            factor_grad(i - 2)
        if i >= 3:
            add_down(i - 3)
    if count >= 3:
        join_down(count - 3)
    scatter_step()
    if count >= 2:
        add_down(count - 2)
    mix_down(count - 1)
    stack_down(count)
    factor_grad(count - 1)
    scatter_step()
    if count >= 2:
        join_down(count - 2)

    backs = [state[c]["back_after"] for c in reversed(steps)]
    mixes = [state[c]["mixed"] for c in reversed(steps)]
    fines = [None] + [state[c]["fine"] for c in reversed(steps[:-1])]
    gain_mlp_sum = sums["gain"]

    flipped = fine_factor.transpose(0, 2, 1)
    grad_in, rest, fine_high, gain_high = tail(
        token_blocks, row_mix, flipped[:, :, width:], backs[1:], mixes[1:], fines[1:], width
    )
    coarse_sum = sums["coarse"]
    valid = (jnp.arange(2 * pair) < pair)[:, None] | (level == depth - 2)
    part = jnp.where(valid & ~spot, coarse_sum, 0.0).astype(BF16)
    part = jnp.einsum("rp,grc->gpc", rows_up, part, preferred_element_type=F32).astype(BF16)
    placed = jnp.einsum("gpc,cq->gpq", part, columns_up, preferred_element_type=F32).astype(BF16)
    cut = HG * NC
    joint = jnp.concatenate([placed.reshape(cut, NC), fine_high.astype(BF16).reshape(-1, NB)])
    joint = reduce_all(joint, ("dp",))
    Order.also(joint)
    add_down(count - 1)
    scatter_step()
    joint = reduce_all(joint, ("seq",), first=planes)
    join_down(count - 1)
    fines[0] = state[count - 1]["fine"]
    grad_in, fine_low, gain_low = last(
        token_blocks, row_mix, flipped[:, :width, :width], backs[0], mixes[0], fines[0], rest, grad_in
    )

    facing = swap(joint)
    coarse_all = jnp.where(
        plane == 0,
        jnp.concatenate([joint[:cut], facing[:cut]]),
        jnp.concatenate([facing[:cut], joint[:cut]]),
    ).astype(F32).reshape(G, NC, NC)
    fine_all = (joint[cut:].astype(F32) + facing[cut:].astype(F32)).reshape(G, -1, NB)
    small = jnp.concatenate(
        [
            fine_low.reshape(-1, D),
            gain_high + gain_low,
            gain_mlp_sum,
        ],
        axis=0,
    )
    small = reduce_all(small, ("dp", "seq"))
    while scatters[0].order or scatters[0].arriving is not None:
        scatter_step()
    weight_grads = jnp.concatenate(
        [part.value.reshape(-1, part.columns) for part in scatters], axis=1
    ).astype(F32)
    low_rows = small[:-2].reshape(G, width, width)
    low_rows = jnp.pad(low_rows, ((0, 0), (0, 0), (0, NB - width)))

    all_seqs = data_devices * tokens.shape[0]
    scale_tokens = 1.0 / math.sqrt(all_seqs * NC * NB)
    grad_fine = jnp.tril(jnp.concatenate([low_rows, fine_all], axis=1))
    grad_fine = grad_fine * (1.0 / math.sqrt(all_seqs * NC * GW))
    grad_coarse = jnp.tril(coarse_all) * (1.0 / math.sqrt(all_seqs * NB * GW))
    return (
        kept[0].reshape(1, rows, D),
        grad_in.reshape(1, rows, D),
        weight_grads[:, :2 * FF] * scale_tokens,
        weight_grads[:, 2 * FF:] * scale_tokens,
        grad_fine,
        grad_coarse,
        small[-2] * scale_tokens,
        small[-1] * scale_tokens,
    )


def solution(mesh):
    placed = (
        P("dp", "seq", None),
        P("dp", "seq", None),
        P(),
        P(),
        P(),
        P(),
        P(("dp", "seq"), None),
        P(("dp", "seq"), None),
    )
    return jax.shard_map(
        on_device,
        mesh=mesh,
        in_specs=placed,
        out_specs=(
            P("dp", "seq", None),
            P("dp", "seq", None),
            P(("dp", "seq"), None),
            P(("dp", "seq"), None),
            P(),
            P(),
            P(),
            P(),
        ),
        check_vma=False,
    )
```

```python
import functools
import math

import jax
import jax.numpy as jnp
from jax import lax
from jax.experimental import pallas as pl
from jax.experimental.pallas import tpu as pltpu
from jax.sharding import PartitionSpec as P

D = 1024
FF = 1024
NB = 128
NC = 128
GW = 128
G = D // GW
HG = G // 2
HALF = D // 2
STRIP = 256

epsilon = 1e-05
F32 = jnp.float32
BF16 = jnp.bfloat16
NT = (((1,), (1,)), ((), ()))
MIB = 1 << 20


def dot(left, right):
    return jnp.dot(left, right, preferred_element_type=F32)


def dot_nt(left, right):
    return lax.dot_general(left, right, NT, preferred_element_type=F32)


def inv_rms(values):
    return lax.rsqrt(jnp.mean(values * values, axis=-1, keepdims=True) + epsilon)


def params(mib):
    return pltpu.CompilerParams(vmem_limit_bytes=mib * MIB)


def cost():
    return pl.CostEstimate(flops=1, bytes_accessed=1, transcendentals=0)


class Order:
    before = []

    @classmethod
    def mark(cls, *values):
        cls.before = list(values)

    @classmethod
    def also(cls, *values):
        cls.before = cls.before + list(values)


def run(kernel, in_specs, operands, **rest):
    extra = Order.before
    count = len(operands)

    def body(*refs):
        kernel(*refs[:count], *refs[count + len(extra):])

    outs = pl.pallas_call(
        body,
        in_specs=list(in_specs) + [pl.BlockSpec(memory_space=pl.ANY)] * len(extra),
        cost_estimate=cost(),
        **rest,
    )(*operands, *extra)
    Order.mark(outs[-1] if isinstance(outs, (list, tuple)) else outs)
    return outs


def lanes_of(blocks, group):
    part = slice(group * GW, (group + 1) * GW)
    return jnp.concatenate([blocks[i, :, part] for i in range(blocks.shape[0])], axis=1)


def spread(rows, plane, own, other, count, width):
    for slot, out in enumerate((own, other)):
        half = plane if slot == 0 else 1 - plane
        for local in range(HG):
            for b in range(width):
                at = (local * width + b) * GW
                took = rows[half * HG + local, pl.ds(b, count, stride=width), :]
                out[:, at:at + GW] = took.astype(BF16)


def collect(rows, plane, own, other, count, width):
    for slot, part in enumerate((own, other)):
        half = plane if slot == 0 else 1 - plane
        for local in range(HG):
            for b in range(width):
                at = (local * width + b) * GW
                took = part[:, at:at + GW].astype(F32)
                rows[half * HG + local, pl.ds(b, count, stride=width), :] = took
    return jnp.concatenate([rows[group] for group in range(G)], axis=1)


def fine_kernel(unit, starts, plane, tok, gain, factor, *refs):
    outs, hidden, rows = refs[:-2], refs[-2], refs[-1]
    count = tok.shape[0]
    low = min(starts)
    span = rows.shape[0] // count
    high = low + span
    for i in range(count):
        source = tok[i].astype(F32)
        hidden[i] = (source * inv_rms(source) * gain[...]).astype(BF16)
    for slot in range(2):
        half = plane[0] if slot == 0 else 1 - plane[0]
        for local in range(HG):
            group = half * HG + local
            lanes = pl.ds(pl.multiple_of(group * GW, GW), GW)
            side = jnp.concatenate([hidden[i, :, lanes] for i in range(count)], axis=1)
            mixed = dot(factor[group, low:high], side)
            for i in range(count):
                rows[i * span:(i + 1) * span, :] = mixed[:, i * GW:(i + 1) * GW]
            for chunk, start in enumerate(starts):
                out = outs[chunk] if slot == 0 else outs[-1]
                units = outs[chunk].shape[1] // (HG * unit * GW)
                skip = chunk * units if slot == 1 else 0
                start -= low
                for u in range(units):
                    for b in range(unit):
                        at = (((skip + u) * HG + local) * unit + b) * GW
                        took = rows[pl.ds(start + u * unit + b, count, stride=span), :]
                        out[:, at:at + GW] = took.astype(BF16)


def fine_forward(plane, tokens, gain, factor, starts, widths, unit):
    blocks = tokens.shape[0]
    shapes = [(blocks, width * HALF) for width in widths]
    shapes.append((blocks, sum(widths) * HALF))
    full = lambda shape: pl.BlockSpec(shape, lambda i: (0,) * len(shape))
    return run(
        functools.partial(fine_kernel, unit, starts),
        grid=(1,),
        in_specs=[
            pl.BlockSpec(memory_space=pltpu.SMEM),
            full((blocks, NB, D)),
            full((1, D)),
            full((G, NB, NB)),
        ],
        out_specs=[full(shape) for shape in shapes],
        out_shape=[jax.ShapeDtypeStruct(shape, BF16) for shape in shapes],
        scratch_shapes=[pltpu.VMEM((blocks, NB, D), BF16), pltpu.VMEM((blocks * sum(widths), GW), F32)],
        compiler_params=params(48),
        operands=[plane, tokens, gain, factor],
        name="fine_forward",
    )


def join_kernel(plane, own, other, out, rows):
    count, width = out.shape[:2]
    out[...] = collect(rows, plane[0], own, other, count, width).astype(BF16).reshape(out.shape)


def join(plane, own, other, unit):
    blocks, lanes = own.shape
    width = lanes // HALF
    half = pl.BlockSpec((blocks, unit * HALF), lambda i: (0, i))
    return run(
        join_kernel,
        grid=(width // unit,),
        in_specs=[pl.BlockSpec(memory_space=pltpu.SMEM), half, half],
        out_specs=pl.BlockSpec((blocks, unit, D), lambda i: (0, i, 0)),
        out_shape=jax.ShapeDtypeStruct((blocks, width, D), BF16),
        scratch_shapes=[pltpu.VMEM((G, blocks * unit, GW), F32)],
        compiler_params=params(24),
        operands=[plane, own, other],
        name="join",
    )


def coarse_kernel(count, *refs):
    weight, base, part = refs[count:]
    stacked = jnp.concatenate([raw[...] for raw in refs[:count]], axis=0)
    high = base.shape[0]
    lanes = base.shape[1] // HG
    for group in range(HG):
        strip = slice(group * lanes, (group + 1) * lanes)
        total = dot(weight[group], stacked[:, strip]).astype(BF16)
        base[:, strip] = total[:high]
        part[:, strip] = total[high:]


def coarse_mix(raws, weight, unit):
    lanes = raws[0].shape[1]
    tile = unit * HALF
    out_rows = weight.shape[1] // 2
    half = pl.BlockSpec((out_rows, tile), lambda t: (0, t))
    return run(
        functools.partial(coarse_kernel, len(raws)),
        grid=(lanes // tile,),
        in_specs=[
            *[pl.BlockSpec((raw.shape[0], tile), lambda t: (0, t)) for raw in raws],
            pl.BlockSpec(weight.shape, lambda t: (0, 0, 0)),
        ],
        out_specs=[half, half],
        out_shape=[jax.ShapeDtypeStruct((out_rows, lanes), BF16)] * 2,
        compiler_params=params(32),
        operands=[*raws, weight],
        name="coarse_mix",
    )


def stack_kernel(flag, own, other, *refs):
    here = jnp.concatenate([own[...], other[...]], axis=0)
    if len(refs) == 1:
        refs[0][...] = here
    else:
        part, leap, out = refs
        out[...] = here
        leap[...] = jnp.where(flag[0] == 1, here, part[...])


def stack(flag, own, other, part, unit, at=0):
    blocks, lanes = own.shape
    tile = unit * HALF
    skip = at * lanes // tile
    half = pl.BlockSpec((blocks, tile), lambda t: (0, t))
    taken = pl.BlockSpec((blocks, tile), lambda t: (0, skip + t))
    whole = pl.BlockSpec((2 * blocks, tile), lambda t: (0, t))
    shape = jax.ShapeDtypeStruct((2 * blocks, lanes), BF16)
    more = [] if part is None else [part]
    outs = run(
        stack_kernel,
        grid=(lanes // tile,),
        in_specs=[pl.BlockSpec(memory_space=pltpu.SMEM), half, taken] + [whole] * len(more),
        out_specs=[whole] * (1 + len(more)),
        out_shape=[shape] * (1 + len(more)),
        compiler_params=params(24),
        operands=[flag, own, other, *more],
        name="stack",
    )
    return outs[-1], outs[0]


def add_kernel(flag, base, extra, own, other):
    count = own.shape[0]
    more = jnp.where(flag[0] == 1, extra[...].astype(F32), 0.0)
    total = (base[...].astype(F32) + more).astype(BF16)
    own[...] = total[:count]
    other[...] = total[count:]


def add_split(flag, base, extra, unit):
    blocks, lanes = base.shape[0] // 2, base.shape[1]
    tile = unit * HALF
    whole = pl.BlockSpec((2 * blocks, tile), lambda t: (0, t))
    half = pl.BlockSpec((blocks, tile), lambda t: (0, t))
    return run(
        add_kernel,
        grid=(lanes // tile,),
        in_specs=[pl.BlockSpec(memory_space=pltpu.SMEM), whole, whole],
        out_specs=[half, half],
        out_shape=[jax.ShapeDtypeStruct((blocks, lanes), BF16)] * 2,
        compiler_params=params(16),
        operands=[flag, base, extra],
        name="add_split",
    )


def coarse_grad_kernel(ups, downs, *refs):
    upper = jnp.concatenate([ref[...] for ref in refs[:ups]], axis=0)
    lower = jnp.concatenate([ref[...] for ref in refs[ups:ups + downs]], axis=0)
    out = refs[-1]
    lanes = upper.shape[1] // HG

    @pl.when(pl.program_id(0) == 0)
    def _():
        out[...] = jnp.zeros_like(out)

    for group in range(HG):
        strip = slice(group * lanes, (group + 1) * lanes)
        out[group] += dot_nt(upper[:, strip], lower[:, strip])


def coarse_grad(uppers, lowers, unit):
    lanes = uppers[0].shape[1]
    tile = unit * HALF
    high = sum(u.shape[0] for u in uppers)
    wide = sum(v.shape[0] for v in lowers)
    return run(
        functools.partial(coarse_grad_kernel, len(uppers), len(lowers)),
        grid=(lanes // tile,),
        in_specs=[pl.BlockSpec((v.shape[0], tile), lambda t: (0, t)) for v in uppers + lowers],
        out_specs=pl.BlockSpec((HG, high, wide), lambda t: (0, 0, 0)),
        out_shape=jax.ShapeDtypeStruct((HG, high, wide), F32),
        compiler_params=params(32),
        operands=[*uppers, *lowers],
        name="coarse_grad",
    )


def mlp_kernel(plane, tok, cot, own, other, gain_mix, gain_mlp, weights, *refs):
    layer, mlp_in, active, back_both, back_after, mixed, back_own, back_other = refs[-10:-2]
    gain_sum, rows = refs[-2:]
    shape = tok.shape
    flat = (shape[0] * shape[1], D)
    taken = collect(rows, plane[0], own, other, shape[0], shape[1])
    mixed[...] = taken.astype(BF16).reshape(shape)
    source = tok[...].reshape(flat).astype(F32)
    hidden = (source * inv_rms(source) * gain_mix[...]).astype(BF16).astype(F32)
    after = source + taken * hidden
    scale = inv_rms(after)
    normed = after * scale
    entering = (normed * gain_mlp[...]).astype(BF16)
    mlp_in[...] = entering.reshape(shape)
    upstream = cot[...].reshape(flat)
    active_parts, gate_parts, up_parts = [], [], []
    for start in range(0, FF, STRIP):
        strip = slice(start, start + STRIP)
        gate = dot(entering, weights[:, strip])
        upward = dot(entering, weights[:, FF + start:FF + start + STRIP])
        back_act = dot(upstream, weights[:, 2 * FF + start:2 * FF + start + STRIP])
        back_act = back_act.astype(BF16).astype(F32)
        squash = jax.nn.sigmoid(gate)
        silu = gate * squash
        slope = squash * (1.0 + gate * (1.0 - squash))
        active_parts.append((silu * upward).astype(BF16))
        gate_parts.append((back_act * upward * slope).astype(BF16))
        up_parts.append((back_act * silu).astype(BF16))
    activation = jnp.concatenate(active_parts, axis=1)
    back_gate = jnp.concatenate(gate_parts, axis=1)
    back_up = jnp.concatenate(up_parts, axis=1)
    active[...] = activation.reshape(shape)
    back_both[:, :, :FF] = back_gate.reshape(shape)
    back_both[:, :, FF:] = back_up.reshape(shape)
    layer[...] = (after + dot_nt(activation, weights[:, 2 * FF:])).astype(BF16).reshape(shape)
    back_in = dot_nt(back_gate, weights[:, :FF]) + dot_nt(back_up, weights[:, FF:2 * FF])

    @pl.when(pl.program_id(0) == 0)
    def _():
        gain_sum[...] = jnp.zeros_like(gain_sum)

    gain_sum[...] += jnp.sum(back_in * normed, axis=0, keepdims=True)
    weighted = back_in * gain_mlp[...]
    centre = jnp.mean(weighted * normed, axis=-1, keepdims=True)
    total = upstream.astype(F32) + scale * (weighted - normed * centre)
    back_after[...] = total.astype(BF16).reshape(shape)
    back_mixed = total * hidden
    for group in range(G):
        rows[group] = back_mixed[:, group * GW:(group + 1) * GW]
    spread(rows, plane[0], back_own, back_other, shape[0], shape[1])


def mlp(plane, tokens, cotangent, own, other, gain_mix, gain_mlp, weights, kept, start, unit):
    blocks, lanes = own.shape
    width = lanes // HALF
    first = start // unit
    whole = pl.BlockSpec((blocks, unit, D), lambda i: (0, first + i, 0))
    local = pl.BlockSpec((blocks, unit, D), lambda i: (0, i, 0))
    half = pl.BlockSpec((blocks, unit * HALF), lambda i: (0, i))
    gain = pl.BlockSpec((1, D), lambda i: (0, 0))
    operands = [plane, tokens, cotangent, own, other, gain_mix, gain_mlp, weights]
    specs = [pl.BlockSpec(memory_space=pltpu.SMEM), whole, whole, half, half, gain, gain]
    specs.append(pl.BlockSpec((D, 3 * FF), lambda i: (0, 0)))
    aliases = {len(operands) + i: i for i in range(len(kept))}
    operands += kept
    specs += [pl.BlockSpec(memory_space=pl.ANY)] * len(kept)
    part = jax.ShapeDtypeStruct((blocks, width, D), BF16)
    full = jax.ShapeDtypeStruct((blocks, NB, D), BF16)
    return run(
        mlp_kernel,
        grid=(width // unit,),
        in_specs=specs,
        out_specs=[
            whole,
            whole,
            whole,
            pl.BlockSpec((blocks, unit, 2 * FF), lambda i: (0, first + i, 0)),
            local,
            local,
            half,
            half,
            gain,
        ],
        out_shape=[
            full,
            full,
            full,
            jax.ShapeDtypeStruct((blocks, NB, 2 * FF), BF16),
            part,
            part,
            jax.ShapeDtypeStruct((blocks, lanes), BF16),
            jax.ShapeDtypeStruct((blocks, lanes), BF16),
            jax.ShapeDtypeStruct((1, D), F32),
        ],
        scratch_shapes=[pltpu.VMEM((G, blocks * unit, GW), F32)],
        input_output_aliases=aliases,
        compiler_params=params(56),
        operands=operands,
        name="mlp",
    )


def weight_kernel(span, bit, mlp_in, active, back_both, cot, *refs):
    outs, total = refs[:-1], refs[-1]
    count = mlp_in.shape[0] * mlp_in.shape[1]
    step, steps = pl.program_id(0), pl.num_programs(0)
    turn = (((0,), (0,)), ((), ()))
    entering = mlp_in[...].reshape(count, D)
    upstream = cot[...].reshape(count, D)

    @pl.when(step == 0)
    def _():
        total[...] = jnp.zeros_like(total)

    for start in range(0, 3 * FF, STRIP):
        if start < 2 * FF:
            left, right = entering, back_both[:, :, start:start + STRIP]
        else:
            left, right = upstream, active[:, :, start - 2 * FF:start - 2 * FF + STRIP]
        total[:, start:start + STRIP] += lax.dot_general(
            left, right.reshape(count, STRIP), turn, preferred_element_type=F32
        )

    @pl.when(step == steps - 1)
    def _():
        for i in range(2):
            keep, away = outs[2 * i], outs[2 * i + 1]
            rows, wide = keep.shape
            columns = slice(i * wide, (i + 1) * wide)
            for at in range(0, rows, span):
                mine = pl.multiple_of(2 * at + bit[0] * span, span)
                theirs = pl.multiple_of(2 * at + (1 - bit[0]) * span, span)
                keep[at:at + span, :] = total[pl.ds(mine, span), columns].astype(BF16)
                away[at:at + span, :] = total[pl.ds(theirs, span), columns].astype(BF16)


def weight_grads_of(kept, cotangent, bit, inner, devices, unit):
    blocks = cotangent.shape[0]
    block = pl.BlockSpec((blocks, unit, D), lambda k: (0, k, 0))
    wide = pl.BlockSpec((blocks, unit, 2 * FF), lambda k: (0, k, 0))
    shape = (D // 2, 3 * FF // 2)
    half = pl.BlockSpec(shape, lambda k: (0, 0))
    return run(
        functools.partial(weight_kernel, inner * D // devices),
        grid=(NB // unit,),
        in_specs=[pl.BlockSpec(memory_space=pltpu.SMEM), block, block, wide, block],
        out_specs=[half] * 4,
        out_shape=[jax.ShapeDtypeStruct(shape, BF16)] * 4,
        scratch_shapes=[pltpu.VMEM((D, 3 * FF), F32)],
        compiler_params=params(56),
        operands=[bit, kept[1], kept[2], kept[3], cotangent],
        name="weight_grad",
    )


def finish(source, gain, back_after, mixed, blocked):
    scale = inv_rms(source)
    normed = source * scale
    back_hidden = back_after * mixed + blocked
    weighted = back_hidden * gain
    centre = jnp.mean(weighted * normed, axis=-1, keepdims=True)
    return back_hidden * normed, back_after + scale * (weighted - normed * centre)


def tail_kernel(count, unit, tok, gain, factor, *refs):
    backs, mixes, fines = (refs[i * count:(i + 1) * count] for i in range(3))
    grad, rest, fine_term, gain_sum, blocked = refs[3 * count:]
    steps = tok.shape[0]

    @pl.when(pl.program_id(0) == 0)
    def _():
        fine_term[...] = jnp.zeros_like(fine_term)
        gain_sum[...] = jnp.zeros_like(gain_sum)

    source = tok[...].astype(F32)
    hidden = (source * inv_rms(source) * gain[...]).astype(BF16)
    back_fine = jnp.concatenate([ref[...] for ref in fines], axis=1)
    for group in range(G):
        upper = lanes_of(back_fine, group)
        result = dot(factor[group], upper)
        for i in range(steps):
            blocked[i, :, group * GW:(group + 1) * GW] = result[:, i * GW:(i + 1) * GW]
        fine_term[group] += dot_nt(upper, lanes_of(hidden, group))
    back_after = jnp.concatenate([ref[...] for ref in backs], axis=1).astype(F32)
    mixed = jnp.concatenate([ref[...] for ref in mixes], axis=1).astype(F32)
    terms, grads = finish(source[:, unit:], gain[...], back_after, mixed, blocked[:, unit:])
    gain_sum[...] += jnp.sum(jnp.sum(terms, axis=0), axis=0, keepdims=True)
    grad[:, unit:] = grads.astype(BF16)
    grad[:, :unit] = jnp.zeros_like(grad[:, :unit])
    rest[...] = blocked[:, :unit]


def tail(tokens, gain, factor, backs, mixes, fines, unit):
    blocks = tokens.shape[0]
    step = min(2, blocks)
    one = pl.BlockSpec((step, NB, D), lambda i: (i, 0, 0))

    def rows(arrays):
        return [pl.BlockSpec((step, v.shape[1], D), lambda i: (i, 0, 0)) for v in arrays]

    return run(
        functools.partial(tail_kernel, len(backs), unit),
        grid=(blocks // step,),
        in_specs=[
            one,
            pl.BlockSpec((1, D), lambda i: (0, 0)),
            pl.BlockSpec(factor.shape, lambda i: (0, 0, 0)),
            *rows(backs),
            *rows(mixes),
            *rows(fines),
        ],
        out_specs=[
            one,
            pl.BlockSpec((step, unit, D), lambda i: (i, 0, 0)),
            pl.BlockSpec((G, NB - unit, NB), lambda i: (0, 0, 0)),
            pl.BlockSpec((1, D), lambda i: (0, 0)),
        ],
        out_shape=[
            jax.ShapeDtypeStruct((blocks, NB, D), BF16),
            jax.ShapeDtypeStruct((blocks, unit, D), F32),
            jax.ShapeDtypeStruct((G, NB - unit, NB), F32),
            jax.ShapeDtypeStruct((1, D), F32),
        ],
        scratch_shapes=[pltpu.VMEM((step, NB, D), F32)],
        compiler_params=params(48),
        operands=[tokens, gain, factor, *backs, *mixes, *fines],
        name="fine_backward",
    )


def last_kernel(tok, gain, factor, back, mix, fine, rest, _, grad, fine_term, gain_sum, blocked):
    blocks = tok.shape[0]
    source = tok[...].astype(F32)
    hidden = (source * inv_rms(source) * gain[...]).astype(BF16)
    back_fine = fine[...]
    for group in range(G):
        upper = lanes_of(back_fine, group)
        result = dot(factor[group], upper)
        for i in range(blocks):
            part = slice(group * GW, (group + 1) * GW)
            blocked[i, :, part] = rest[i, :, part] + result[:, i * GW:(i + 1) * GW]
        fine_term[group] = dot_nt(upper, lanes_of(hidden, group))
    terms, grads = finish(source, gain[...], back[...].astype(F32), mix[...].astype(F32), blocked[...])
    gain_sum[...] = jnp.sum(jnp.sum(terms, axis=0), axis=0, keepdims=True)
    grad[...] = grads.astype(BF16)


def last(tokens, gain, factor, back, mix, fine, rest, grad):
    blocks, unit = back.shape[:2]
    one = pl.BlockSpec((blocks, unit, D), lambda i: (0, 0, 0))
    return run(
        last_kernel,
        grid=(1,),
        in_specs=[
            one,
            pl.BlockSpec((1, D), lambda i: (0, 0)),
            pl.BlockSpec(factor.shape, lambda i: (0, 0, 0)),
            one,
            one,
            one,
            one,
            pl.BlockSpec(memory_space=pl.ANY),
        ],
        out_specs=[
            one,
            pl.BlockSpec((G, unit, unit), lambda i: (0, 0, 0)),
            pl.BlockSpec((1, D), lambda i: (0, 0)),
        ],
        out_shape=[
            jax.ShapeDtypeStruct(grad.shape, BF16),
            jax.ShapeDtypeStruct((G, unit, unit), F32),
            jax.ShapeDtypeStruct((1, D), F32),
        ],
        input_output_aliases={7: 0},
        scratch_shapes=[pltpu.VMEM((blocks, unit, D), F32)],
        compiler_params=params(48),
        operands=[tokens, gain, factor, back, mix, fine, rest, grad],
        name="fine_backward_last",
    )


def reduce_all(value, axes, first=1):
    for axis in axes:
        size = lax.axis_size(axis)
        reach = first
        while reach < size:
            pairs = [(i, i ^ reach) for i in range(size)]
            value = value + lax.ppermute(value, axis, pairs)
            reach *= 2
    return value


def split_kernel(inner, has_arrived, bit, value, *refs):
    keep, away = refs[-2:]
    side = bit[0]
    for j in range(keep.shape[0]):
        base = j // inner * 2 * inner + j % inner
        mine, theirs = base + side * inner, base + (1 - side) * inner
        if has_arrived:
            keep[j] = value[mine] + refs[0][mine]
            away[j] = value[theirs] + refs[0][theirs]
        else:
            keep[j] = value[mine]
            away[j] = value[theirs]


def split(bit, value, arrived, inner):
    shape = (value.shape[0] // 2,) + value.shape[1:]
    full = lambda shape: pl.BlockSpec(shape, lambda i: (0,) * len(shape))
    more = [] if arrived is None else [arrived]
    return run(
        functools.partial(split_kernel, inner, bool(more)),
        grid=(1,),
        in_specs=[pl.BlockSpec(memory_space=pltpu.SMEM)] + [full(value.shape)] * (1 + len(more)),
        out_specs=[full(shape)] * 2,
        out_shape=[jax.ShapeDtypeStruct(shape, BF16)] * 2,
        compiler_params=params(32),
        operands=[bit, value, *more],
        name="split",
    )


class Scatter:

    def __init__(self, late):
        bits = []
        for axis in ("dp", "seq"):
            size = lax.axis_size(axis)
            bits += [(axis, 1 << k) for k in reversed(range(size.bit_length() - 1))]
        outer = [bit for bit in reversed(bits) if bit[0] == "dp"]
        inner = [bit for bit in reversed(bits) if bit[0] == "seq"]
        self.order = outer[:1] + inner[:1] + outer[1:] + inner[1:] if late else outer + inner
        self.left = bits
        self.next()

    def next(self):
        self.axis, self.reach = self.order.pop(0)
        at = self.left.index((self.axis, self.reach))
        self.left = self.left[:at] + self.left[at + 1:]
        self.inner = 2 ** (len(self.left) - at)
        self.bit = ((lax.axis_index(self.axis) // self.reach) % 2).astype(jnp.int32).reshape(1)

    def send(self, keep, away):
        size = lax.axis_size(self.axis)
        pairs = [(i, i ^ self.reach) for i in range(size)]
        self.value, self.arriving = keep, lax.ppermute(away, self.axis, pairs)

    def step(self):
        if not self.order:
            self.value, self.arriving = self.value + self.arriving, None
            return
        self.next()
        self.send(*split(self.bit, self.value, self.arriving, self.inner))


def assemble_kernel(spots, bit, mine, theirs, out):
    side = bit[0]
    for j in range(mine.shape[0]):
        low, high = spots[j]
        out[low] = jnp.where(side == 0, mine[j], theirs[j])
        out[high] = jnp.where(side == 0, theirs[j], mine[j])


def assemble(bit, mine, theirs, spots):
    full = lambda shape: pl.BlockSpec(shape, lambda i: (0,) * len(shape))
    shape = (2 * mine.shape[0],) + mine.shape[1:]
    return run(
        functools.partial(assemble_kernel, spots),
        grid=(1,),
        in_specs=[pl.BlockSpec(memory_space=pltpu.SMEM), full(mine.shape), full(theirs.shape)],
        out_specs=full(shape),
        out_shape=jax.ShapeDtypeStruct(shape, BF16),
        compiler_params=params(48),
        operands=[bit, mine, theirs],
        name="assemble",
    )


class Gather:

    def __init__(self, value):
        self.steps = []
        for axis in ("seq", "dp"):
            size = lax.axis_size(axis)
            reaches = [1 << k for k in range(size.bit_length() - 1)]
            self.steps += [(axis, reach) for reach in reversed(reaches)]
        self.value = value[None]
        self.at = 0
        self.send()

    def send(self):
        axis, reach = self.steps[self.at]
        pairs = [(i, i ^ reach) for i in range(lax.axis_size(axis))]
        self.other = lax.ppermute(self.value, axis, pairs)
        self.bit = (lax.axis_index(axis) // reach % 2).astype(jnp.int32).reshape(1)

    def step(self):
        count = self.value.shape[0]
        self.at += 1
        if self.at < len(self.steps):
            spots = [(j, j + count) for j in range(count)]
            self.value = assemble(self.bit, self.value, self.other, spots)
            self.send()
            return
        seq_bits = lax.axis_size("seq").bit_length() - 1
        weigh = [reach << (seq_bits if axis == "dp" else 0) for axis, reach in self.steps]
        spots = []
        for j in range(count):
            low = sum(weight for k, weight in enumerate(weigh[:-1]) if j >> k & 1)
            spots.append((low, low + weigh[-1]))
        self.value = assemble(self.bit, self.value, self.other, spots)

    def finish(self):
        while self.at < len(self.steps):
            self.step()
        return self.value.reshape(-1, self.value.shape[-1])


def on_device(tokens, cotangent, gain_mix, gain_mlp, fine_factor, coarse_factor, w_gate_up, w_down):
    rows = tokens.shape[1]
    blocks = rows // NB
    seq_devices = lax.axis_size("seq")
    data_devices = lax.axis_size("dp")
    planes = 2
    depth = seq_devices // planes
    index = lax.axis_index("seq")
    level, plane = index // planes, index % planes
    unit = max(16, 256 // blocks)
    width = min(2 * unit, NB // 2)
    widths = [width] * (NB // width)

    def shift(value, by, low=0, high=None):
        top = depth - 1 if high is None else high
        pairs = [
            (lv * planes + p, (lv + by) * planes + p)
            for lv in range(depth)
            for p in range(planes)
            if low <= lv + by <= top
        ]
        return lax.ppermute(value, "seq", pairs)

    def swap(value):
        return lax.ppermute(value, "seq", [(i, i ^ 1) for i in range(seq_devices)])

    gathered = Gather(jnp.concatenate([w_gate_up, w_down], axis=1))
    token_blocks = tokens.reshape(blocks, NB, D)
    cot_blocks = cotangent.reshape(blocks, NB, D)
    row_mix, row_mlp = gain_mix.reshape(1, D), gain_mlp.reshape(1, D)

    pair = planes * blocks
    local = jnp.arange(pair)
    order = jnp.where(plane == 0, local, (local + blocks) % pair)

    def picks(*levels):
        wanted = jnp.concatenate([order + lv * pair for lv in levels])
        return (wanted[:, None] == jnp.arange(NC)[None, :]).astype(BF16)

    reaches = list(range(max(2, depth - 1)))
    far = reaches[-1]
    up_levels = [level - d for d in reaches[:-1]] + [jnp.where(level == far, 0, depth)]
    down_levels = [level + d for d in reaches[:-1]] + [jnp.where(level == 1, depth - 1, depth)]
    rows_up, columns_up = picks(level, level + 1), picks(*up_levels)
    rows_down, columns_down = picks(level, level - 1), picks(*down_levels)
    spot = (jnp.arange(2 * pair)[:, None] >= pair) & (jnp.arange(len(reaches) * pair)[None] < pair)
    factor = lax.dynamic_slice_in_dim(coarse_factor, plane * HG, HG, axis=0)

    def chosen(matrix, rows_of, columns_of):
        some = jnp.einsum("rp,gpq->grq", rows_of, matrix, preferred_element_type=F32)
        some = jnp.einsum(
            "grq,cq->grc", some.astype(BF16), columns_of, preferred_element_type=F32
        )
        return jnp.where(spot, 0.0, some).astype(BF16)

    which = plane.reshape(1).astype(jnp.int32)
    count = len(widths)
    starts = [NB - sum(widths[:i + 1]) for i in range(count)]
    steps = range(count)
    state = [dict() for _ in steps]
    kept = []
    sums = {}
    Order.mark()

    def forward(*chunks):
        outs = fine_forward(
            which, token_blocks, row_mix, fine_factor,
            [starts[c] for c in chunks], [widths[c] for c in chunks], unit,
        )
        arrived = swap(outs[-1])
        for at, c in enumerate(chunks):
            state[c]["pair"] = outs[at], arrived, at

    last_flag = (level == depth - 1).astype(jnp.int32).reshape(1)
    first_flag = (level == 0).astype(jnp.int32).reshape(1)

    def leap_up(value, raw, part):
        pairs = []
        for p in range(planes):
            pairs += [(p, far * planes + p)] if raw else []
            pairs += [(far * planes + p, (depth - 1) * planes + p)] if part else []
        return lax.ppermute(value, "seq", pairs)

    def leap_down(value, raw, part):
        pairs = []
        for p in range(planes):
            pairs += [((depth - 1) * planes + p, planes + p)] if raw else []
            pairs += [(planes + p, p)] if part else []
        return lax.ppermute(value, "seq", pairs)

    def stack_up(c):
        part = state[c - 1]["part"] if c > 0 else None
        if c < count:
            own, other, at = state[c]["pair"]
            here, leap = stack(first_flag, own, other, part, unit, at)
            middle = [shift(here, d, high=depth - 2) for d in reaches[2:-1]]
            raws = [here, shift(here, 1)] + middle
        else:
            leap = part
        leap = leap_up(leap, c < count, c > 0)
        if c > 0:
            state[c - 1]["extra"] = leap
        if c < count:
            state[c]["raws"] = raws + [leap]

    def mix_up(c):
        state[c]["base"], state[c]["part"] = coarse_mix(state[c]["raws"], up_weight, unit)

    def add_up(c):
        own, other = add_split(last_flag, state[c]["base"], state[c]["extra"], unit)
        state[c]["own"], state[c]["other"] = own, swap(other)

    def run_mlp(c, kept):
        outs = mlp(
            which, token_blocks, cot_blocks, state[c]["own"], state[c]["other"], row_mix, row_mlp,
            gathered.finish(), kept, starts[c], unit,
        )
        names = ["back_after", "mixed", "down_own", "down_other"]
        state[c].update(zip(names, outs[4:8]))
        sums["gain"] = outs[8] if c == 0 else sums["gain"] + outs[8]
        state[c]["down_other"] = swap(state[c]["down_other"])
        return list(outs[:4])

    def weight_grad():
        parts = [Scatter(False), Scatter(True)]
        first = parts[0]
        outs = weight_grads_of(
            kept, cot_blocks, first.bit, first.inner, data_devices * seq_devices, unit
        )
        for i, part in enumerate(parts):
            shape = (data_devices * seq_devices // 2, -1, 3 * FF // 2)
            part.send(outs[2 * i].reshape(shape), outs[2 * i + 1].reshape(shape))
        return parts

    def stack_down(c):
        part = state[c - 1]["part"] if c > 0 else None
        if c < count:
            own, other = state[c]["down_own"], state[c]["down_other"]
            here, leap = stack(last_flag, own, other, part, unit)
            middle = [shift(here, -d, low=1) for d in reaches[2:-1]]
            backs = [here, shift(here, -1)] + middle
        else:
            leap = part
        leap = leap_down(leap, c < count, c > 0)
        if c > 0:
            state[c - 1]["extra"] = leap
        if c < count:
            state[c]["backs"] = backs + [leap]

    def mix_down(c):
        state[c]["base"], state[c]["part"] = coarse_mix(state[c]["backs"], down_weight, unit)

    def add_down(c):
        own, other = add_split(first_flag, state[c]["base"], state[c]["extra"], unit)
        state[c]["fine_own"], state[c]["fine_other"] = own, swap(other)

    def factor_grad(c):
        part = coarse_grad(state[c]["backs"][:2], state[c]["raws"], unit)
        sums["coarse"] = part if c == 0 else sums["coarse"] + part

    def join_down(c):
        state[c]["fine"] = join(which, state[c]["fine_own"], state[c]["fine_other"], unit)

    def scatter_step():
        for part in scatters:
            part.step()

    up_weight = chosen(factor, rows_up, columns_up)
    down_weight = chosen(factor.transpose(0, 2, 1), rows_down, columns_down)
    forward(0)
    forward(*steps[1:])
    stack_up(0)
    while gathered.at < len(gathered.steps) - 3:
        gathered.step()
    for i in range(count + 1):
        if i >= 1:
            add_up(i - 1)
        if i == 1:
            Order.also(state[0]["other"])
        if i < count:
            mix_up(i)
            stack_up(i + 1)
        if i < 2 and gathered.at < len(gathered.steps) - 1:
            gathered.step()
        if i >= 3:
            mix_down(i - 3)
        if i >= 2:
            stack_down(i - 2)
        if i >= 3:
            factor_grad(i - 3)
        if i >= 1:
            kept = run_mlp(i - 1, kept)
        if i >= 4:
            add_down(i - 4)
    scatters = weight_grad()
    if count >= 2:
        mix_down(count - 2)
    if count >= 3:
        add_down(count - 3)
    stack_down(count - 1)
    if count >= 2:
        factor_grad(count - 2)
    if count >= 4:
        join_down(count - 4)
    scatter_step()
    mix_down(count - 1)
    stack_down(count)
    if count >= 2:
        add_down(count - 2)
    scatter_step()
    factor_grad(count - 1)
    if count >= 3:
        join_down(count - 3)
    if count >= 2:
        join_down(count - 2)

    backs = [state[c]["back_after"] for c in reversed(steps)]
    mixes = [state[c]["mixed"] for c in reversed(steps)]
    fines = [None] + [state[c]["fine"] for c in reversed(steps[:-1])]
    gain_mlp_sum = sums["gain"]

    flipped = fine_factor.transpose(0, 2, 1)
    grad_in, rest, fine_high, gain_high = tail(
        token_blocks, row_mix, flipped[:, :, width:], backs[1:], mixes[1:], fines[1:], width
    )
    coarse_sum = sums["coarse"]
    valid = (jnp.arange(2 * pair) < pair)[:, None] | (level == depth - 2)
    part = jnp.where(valid & ~spot, coarse_sum, 0.0).astype(BF16)
    part = jnp.einsum("rp,grc->gpc", rows_up, part, preferred_element_type=F32).astype(BF16)
    placed = jnp.einsum("gpc,cq->gpq", part, columns_up, preferred_element_type=F32).astype(BF16)
    cut = HG * NC
    joint = jnp.concatenate([placed.reshape(cut, NC), fine_high.astype(BF16).reshape(-1, NB)])
    joint = reduce_all(joint, ("dp",))
    add_down(count - 1)
    scatter_step()
    Order.also(joint)
    joint = reduce_all(joint, ("seq",), first=planes)
    join_down(count - 1)
    scatter_step()
    fines[0] = state[count - 1]["fine"]
    grad_in, fine_low, gain_low = last(
        token_blocks, row_mix, flipped[:, :width, :width], backs[0], mixes[0], fines[0], rest, grad_in
    )

    facing = swap(joint)
    coarse_all = jnp.where(
        plane == 0,
        jnp.concatenate([joint[:cut], facing[:cut]]),
        jnp.concatenate([facing[:cut], joint[:cut]]),
    ).astype(F32).reshape(G, NC, NC)
    fine_all = (joint[cut:].astype(F32) + facing[cut:].astype(F32)).reshape(G, -1, NB)
    small = jnp.concatenate(
        [
            fine_low.reshape(-1, D),
            gain_high + gain_low,
            gain_mlp_sum,
        ],
        axis=0,
    )
    small = reduce_all(small, ("dp", "seq"))
    while scatters[0].order or scatters[0].arriving is not None:
        scatter_step()
    weight_grads = jnp.concatenate(
        [part.value.reshape(-1, 3 * FF // 2) for part in scatters], axis=1
    ).astype(F32)
    low_rows = small[:-2].reshape(G, width, width)
    low_rows = jnp.pad(low_rows, ((0, 0), (0, 0), (0, NB - width)))

    all_seqs = data_devices * tokens.shape[0]
    scale_tokens = 1.0 / math.sqrt(all_seqs * NC * NB)
    grad_fine = jnp.tril(jnp.concatenate([low_rows, fine_all], axis=1))
    grad_fine = grad_fine * (1.0 / math.sqrt(all_seqs * NC * GW))
    grad_coarse = jnp.tril(coarse_all) * (1.0 / math.sqrt(all_seqs * NB * GW))
    return (
        kept[0].reshape(1, rows, D),
        grad_in.reshape(1, rows, D),
        weight_grads[:, :2 * FF] * scale_tokens,
        weight_grads[:, 2 * FF:] * scale_tokens,
        grad_fine,
        grad_coarse,
        small[-2] * scale_tokens,
        small[-1] * scale_tokens,
    )


def solution(mesh):
    placed = (
        P("dp", "seq", None),
        P("dp", "seq", None),
        P(),
        P(),
        P(),
        P(),
        P(("dp", "seq"), None),
        P(("dp", "seq"), None),
    )
    return jax.shard_map(
        on_device,
        mesh=mesh,
        in_specs=placed,
        out_specs=(
            P("dp", "seq", None),
            P("dp", "seq", None),
            P(("dp", "seq"), None),
            P(("dp", "seq"), None),
            P(),
            P(),
            P(),
            P(),
        ),
        check_vma=False,
    )
```
